32 devices in a mesh: pb: 8 (over z, core), pa: 4 (over y, x).
Axes of the slice: x: 2, y: 2, z: 4, core: 2. Of those that a mesh axis runs over, the one named last changes fastest.
Arguments:
- queries: float32 [4096, 1024], P(('pb', 'pa')), may hold values from -2 to 2
- passages: float32 [2048, 1024], P(('pa', 'pb')), may hold values from -2 to 2
- positive: int32 [4096], P('pb'), may hold values from 0 to 2047
Outputs:
- losses: float32 [4096], P('pb')
- query_grad: float32 [4096, 1024], P(('pb', 'pa'))
- passage_grad: float32 [2048, 1024], P(('pa', 'pb'))
The draws below stay inside these ranges and needn't reach their ends.
All inputs are finite; a program needn't handle non-finite values.
Results may differ from the reference program's by a relative error of at most 0.0003.
Values sent between devices are 32-bit elements; how exact they have to be, the bound alone decides.
No kernel may reach another device: no remote copies, remote signals or barrier semaphores. Data moves between devices by JAX's collectives and lax.ppermute only.
A program may use at most 64 MiB of HBM per device.

```python
import math
import jax
import jax.numpy as jnp
from jax import lax

D = 1024
QUERIES = 4096
PASSAGES = 2048


def unit_rows(key, shape):
    return jnp.clip(jax.random.normal(key, shape, jnp.float32), -4.0, 4.0) / math.sqrt(D)


def row_scales(key, count, scale_low, scale_high):
    return jnp.exp(jax.random.uniform(key, (count, 1), jnp.float32, math.log(scale_low), math.log(scale_high)))


def pick_positive(key):
    chosen = jax.random.randint(jax.random.fold_in(key, 101), (QUERIES,), 0, PASSAGES, dtype=jnp.int32)
    first_spot = jax.random.randint(jax.random.fold_in(key, 102), (), 0, QUERIES, dtype=jnp.int32)
    second_spot = (first_spot + 1) % QUERIES
    chosen = chosen.at[first_spot].set(PASSAGES - 1)
    chosen = chosen.at[second_spot].set(0)
    return chosen


def passage_base(key, shared_weight, center_weight):
    groups = max(2, PASSAGES // 128)
    shared = unit_rows(jax.random.fold_in(key, 201), (1, D))
    centers = unit_rows(jax.random.fold_in(key, 202), (groups, D))
    labels = jax.random.randint(jax.random.fold_in(key, 203), (PASSAGES,), 0, groups, dtype=jnp.int32)
    noise_rows = unit_rows(jax.random.fold_in(key, 204), (PASSAGES, D))
    return shared_weight * shared + center_weight * jnp.take(centers, labels, axis=0) + 0.6 * noise_rows


def draw_passages(key, part):
    base_rows = passage_base(key, 0.5, 0.6)
    scale_low, scale_high = (0.5, 2.0)
    key = jax.random.fold_in(key, 3)
    values = base_rows * row_scales(key, PASSAGES, scale_low, scale_high)
    return jnp.clip(values, -2.0, 2.0)


def draw_queries(key, part):
    base_rows = passage_base(key, 0.5, 0.6)
    cos_low, cos_high, scale_low, scale_high = (0.5, 0.9, 0.5, 2.0)
    chosen = pick_positive(key)
    key = jax.random.fold_in(key, 5)
    closeness = jax.random.uniform(jax.random.fold_in(key, 1), (QUERIES, 1), jnp.float32, cos_low, cos_high)
    noise_rows = unit_rows(jax.random.fold_in(key, 2), (QUERIES, D))
    mixed_rows = closeness * jnp.take(base_rows, chosen, axis=0) + jnp.sqrt(1.0 - closeness * closeness) * noise_rows
    values = mixed_rows * row_scales(jax.random.fold_in(key, 3), QUERIES, scale_low, scale_high)
    return jnp.clip(values, -2.0, 2.0)


def draw_positive(key, part):
    return pick_positive(key)


def setup_inputs(seed: int = 0) -> dict:
    key_list = jax.random.split(jax.random.key(seed), 4)
    return {
        "queries": draw_queries(jax.random.fold_in(key_list[3], 71), 0),
        "passages": draw_passages(jax.random.fold_in(key_list[3], 71), 0),
        "positive": draw_positive(jax.random.fold_in(key_list[3], 71), 0),
    }


inv_temp = 20.0

def normalize(rows):
    scale = lax.rsqrt(lax.optimization_barrier(jnp.sum(rows * rows, axis=1, keepdims=True)) + 1e-06)
    return (rows * scale, scale)

def reference(queries, passages, positive):
    qn, rq = normalize(queries)
    pn, rp = normalize(passages)
    block = min(512, QUERIES)
    count = QUERIES // block
    q_blocks = qn.reshape(count, block, D)
    pos_blocks = positive.reshape(count, block)
    columns = jnp.arange(PASSAGES, dtype=jnp.int32)

    def step(carry, item):
        q_block, pos_block = item
        scores = inv_temp * lax.dot_general(q_block, pn, (((1,), (1,)), ((), ())), precision=lax.Precision.HIGHEST, preferred_element_type=jnp.float32)
        expo = jnp.exp(scores)
        total = lax.optimization_barrier(jnp.sum(expo, axis=1))
        onehot = (pos_block[:, None] == columns[None, :]).astype(jnp.float32)
        spos = lax.optimization_barrier(jnp.sum(onehot * scores, axis=1))
        loss = jnp.log(total) - spos
        dscores = expo / total[:, None] - onehot
        gq = inv_temp * jnp.dot(dscores, pn, precision=lax.Precision.HIGHEST, preferred_element_type=jnp.float32)
        gp = inv_temp * lax.dot_general(dscores, q_block, (((0,), (0,)), ((), ())), precision=lax.Precision.HIGHEST, preferred_element_type=jnp.float32)
        return (carry + gp, (loss, gq))
    gp, (losses, gq) = lax.scan(step, jnp.zeros((PASSAGES, D), jnp.float32), (q_blocks, pos_blocks))
    losses = losses.reshape(QUERIES)
    gq = gq.reshape(QUERIES, D)
    query_grad = rq * (gq - qn * lax.optimization_barrier(jnp.sum(qn * gq, axis=1, keepdims=True)))
    passage_grad = rp * (gp - pn * lax.optimization_barrier(jnp.sum(pn * gp, axis=1, keepdims=True)))
    return (losses, query_grad, passage_grad)
```

```python
import functools

import jax
import jax.numpy as jnp
from jax import lax
from jax.experimental import pallas as pl
from jax.experimental.pallas import tpu as pltpu
from jax.sharding import PartitionSpec as P

inv_temp = 20.0
f32 = jnp.float32
bf16 = jnp.bfloat16
AXES = ("pb", "pa")


def call(kernel, outs, flops, *args):
    return pl.pallas_call(
        kernel,
        out_shape=[jax.ShapeDtypeStruct(s, d) for s, d in outs],
        compiler_params=pltpu.CompilerParams(vmem_limit_bytes=40 * 1024 * 1024),
        cost_estimate=pl.CostEstimate(flops=flops, bytes_accessed=8 << 20, transcendentals=0),
    )(*args)


def split(x):
    hi = x.astype(bf16)
    return hi, (x - hi.astype(f32)).astype(bf16)


def mm(a, b, dims):
    return lax.dot_general(a, b, (dims, ((), ())), preferred_element_type=f32)


def mm3(a, b, dims):
    (ah, al), (bh, bl) = a, b
    return mm(al, bh, dims) + mm(ah, bl, dims) + mm(ah, bh, dims)


def normalize(rows):
    scale = lax.rsqrt(jnp.sum(rows * rows, axis=1, keepdims=True) + 1e-06)
    return rows * scale, scale


def onehot(pos_ref, shape):
    return lax.broadcasted_iota(jnp.int32, shape, 0) == pos_ref[...]


def combine(stats):
    n = stats[0].shape[1] // len(stats)
    blocks = [sum(r[:, (m ^ k) * n : (m ^ k) * n + n] for k, r in enumerate(stats)) for m in range(len(stats))]
    return jnp.concatenate(blocks, axis=1)


def scores_kernel(n_q, n_p, *refs):
    qs, ps = refs[:n_q], refs[n_q : n_q + n_p]
    pos, et, stats, qh, ql, ph, pl_ = refs[n_q + n_p :]
    for parts, hi, lo in ((qs, qh, ql), (ps, ph, pl_)):
        at = 0
        for r in parts:
            n = r.shape[0]
            hi[at : at + n], lo[at : at + n] = split(normalize(r[...])[0])
            at += n
    st = inv_temp * mm3((ph[...], pl_[...]), (qh[...], ql[...]), ((1,), (1,)))
    e = jnp.exp(st)
    et[...] = e
    stats[...] = jnp.zeros(stats.shape, f32)
    stats[0:1] = jnp.sum(e, axis=0, keepdims=True)
    stats[1:2] = jnp.sum(jnp.where(onehot(pos, st.shape), st, 0.0), axis=0, keepdims=True)


def unscaled_kernel(et, pos, ph, pl_, u, v):
    p = (ph[...], pl_[...])
    u[...] = mm3(split(et[...].T), p, ((1,), (0,)))
    o = onehot(pos, et.shape).astype(f32).T.astype(bf16)
    v[...] = mm(o, p[1], ((1,), (0,))) + mm(o, p[0], ((1,), (0,)))


def passage_kernel(n_stats, *refs):
    stats = refs[:n_stats]
    et, pos, qh, ql, gp = refs[n_stats:]
    total = combine(stats)[0:1]
    dt = et[...] * (1.0 / total) - onehot(pos, et.shape).astype(f32)
    gp[...] = mm3(split(dt), (qh[...], ql[...]), ((1,), (0,)))


def query_kernel(n_stats, cuts, *refs):
    stats = refs[:n_stats]
    u, v, losses = refs[n_stats : n_stats + 3]
    outs = refs[n_stats + 3 :]
    both = combine(stats)
    losses[...] = jnp.log(both[0:1]) - both[1:2]
    inv = (1.0 / both).T[:, 0:1]
    at = 0
    for out, n in zip(outs, cuts):
        out[...] = u[at : at + n] * inv[at : at + n] - v[at : at + n]
        at += n


def final_kernel(*refs):
    rows, parts, out = refs[0], refs[1:-1], refs[-1]
    xn, scale = normalize(rows[...])
    g = None
    for group in parts:
        g = group[...] if g is None else g + group[...]
    g = inv_temp * g
    out[...] = scale * (g - xn * jnp.sum(xn * g, axis=1, keepdims=True))


def flip(x, mask, only=None):
    n = lax.axis_size("pb") * lax.axis_size("pa")
    pairs = [(i, i ^ mask) for i in range(n) if only is None or only(i)]
    return lax.ppermute(x, AXES, pairs)


X, Y, C, Z1, Z2, Z3 = 1, 2, 4, 8, 16, 24


def middle(i):
    return (i // 8) in (1, 2)


def ends(i):
    return not middle(i)


def rows_of(x, *cuts):
    at, out = 0, []
    for n in cuts:
        out.append(lax.slice_in_dim(x, at, at + n, axis=0))
        at += n
    return out


def small_body(queries, passages, positive):
    qr, pr = queries.shape[0], passages.shape[0]
    h = qr // 2
    q_rows, p_rows = 4 * qr, 8 * pr
    pa, pb = lax.axis_index("pa"), lax.axis_index("pb")

    qa, qb = rows_of(queries, h, h)
    xa, yb = flip(qa, X), flip(qb, Y)
    xb, ya = flip(qb, X), flip(qa, Y)
    da, db = flip(xa, Y), flip(yb, X)
    z2 = flip(passages, Z2)
    z1 = flip(passages, Z1)
    pc = flip(passages, C)
    mid = flip(passages, Z3, middle)
    far = flip(z2, Z1, middle)
    z3 = mid + far
    z1c, z2c, z3c = flip(z1, C), flip(z2, C), flip(z3, C)
    q_parts = [qa, qb, xa, xb, ya, yb, da, db]
    p_parts = [passages, pc, z1, z1c, z2, z2c, z3, z3c]

    order = jnp.arange(4, dtype=jnp.int32) ^ pa
    pos = positive.reshape(4, qr)[order].reshape(1, q_rows)
    pos = jnp.where(pos // p_rows == pa, (pos % p_rows) ^ (pb * pr), -1)

    et, stats, qh, ql, ph, pl_ = scores(q_parts, p_parts, pos)
    both = [stats, flip(stats, X), flip(stats, Y), flip(stats, X + Y)]
    u, v = unscaled(et, pos, ph, pl_)
    gp = passage_grads(both, et, pos, qh, ql)
    losses, own, gxa, gxb, gya, gyb, gda, gdb = query_grads(both, u, v, (qr,) + (h,) * 6)

    fa, fb = flip(gda, X), flip(gdb, Y)
    rxa, ryb = flip(gxa, X), flip(gyb, Y)
    rxb, rya = flip(gxb + fb, X), flip(gya + fa, Y)

    g0, c0, g1, c1, g2, c2, g3, c3 = rows_of(gp, *([pr] * 8))
    g3 = g3 + flip(c3, C)
    ff = flip(g3, Z1, ends)
    g1 = g1 + flip(c1, C)
    g2 = g2 + flip(c2, C)
    rmid = flip(g3, Z3, middle)
    r1 = flip(g1, Z1)
    r2 = flip(g2 + ff, Z2)
    r0 = flip(c0, C)

    losses = losses.reshape(4, qr)[order].reshape(q_rows)
    query_grad = finish(queries, own, jnp.concatenate([rxa, rxb]), jnp.concatenate([rya, ryb]))
    passage_grad = finish(passages, g0, r0, r1, rmid, r2)
    return losses, query_grad, passage_grad


def scores(q_parts, p_parts, pos):
    q_rows, p_rows = sum(x.shape[0] for x in q_parts), sum(x.shape[0] for x in p_parts)
    d = q_parts[0].shape[1]
    return call(
        functools.partial(scores_kernel, len(q_parts), len(p_parts)),
        [((p_rows, q_rows), f32), ((8, q_rows), f32), ((q_rows, d), bf16), ((q_rows, d), bf16), ((p_rows, d), bf16), ((p_rows, d), bf16)],
        6 * q_rows * p_rows * d,
        *q_parts,
        *p_parts,
        pos,
    )


def unscaled(et, pos, ph, pl_):
    p_rows, q_rows = et.shape
    d = ph.shape[1]
    return call(unscaled_kernel, [((q_rows, d), f32)] * 2, 10 * q_rows * p_rows * d, et, pos, ph, pl_)


def passage_grads(both, et, pos, qh, ql):
    p_rows, q_rows = et.shape
    d = qh.shape[1]
    return call(functools.partial(passage_kernel, len(both)), [((p_rows, d), f32)], 6 * q_rows * p_rows * d, *both, et, pos, qh, ql)[0]


def query_grads(both, u, v, cuts):
    q_rows, d = u.shape
    return call(
        functools.partial(query_kernel, len(both), cuts),
        [((1, q_rows), f32)] + [((n, d), f32) for n in cuts],
        3 * q_rows * d,
        *both,
        u,
        v,
    )


def finish(rows, *parts):
    return call(final_kernel, [(rows.shape, f32)], 12 * rows.size, rows, *parts)[0]


def body(queries, passages, positive):
    qr, pr = queries.shape[0], passages.shape[0]
    pa = lax.axis_index("pa")
    q_full = lax.all_gather(queries, "pa", axis=0, tiled=True)
    p_full = lax.all_gather(passages, "pb", axis=0, tiled=True)
    p_rows = p_full.shape[0]
    pos = positive - pa * p_rows
    pos = jnp.where((pos >= 0) & (pos < p_rows), pos, -1).reshape(1, -1)
    et, stats, qh, ql, ph, pl_ = scores([q_full], [p_full], pos)
    both = [lax.psum(stats, "pa")]
    u, v = unscaled(et, pos, ph, pl_)
    gp = passage_grads(both, et, pos, qh, ql)
    losses, gq = query_grads(both, u, v, (q_full.shape[0],))
    q_part = lax.psum_scatter(gq, "pa", scatter_dimension=0, tiled=True)
    p_part = lax.psum_scatter(gp, "pb", scatter_dimension=0, tiled=True)
    return losses.reshape(-1), finish(queries, q_part), finish(passages, p_part)


def solution(mesh):
    placed = (P(("pb", "pa"), None), P(("pa", "pb"), None), P("pb"))
    small = mesh.shape["pa"] == 4 and mesh.shape["pb"] == 8
    return jax.shard_map(
        small_body if small else body,
        mesh=mesh,
        in_specs=placed,
        out_specs=(P("pb"), P(("pb", "pa"), None), P(("pa", "pb"), None)),
        check_vma=False,
    )
```

```python
import functools

import jax
import jax.numpy as jnp
from jax import lax
from jax.experimental import pallas as pl
from jax.experimental.pallas import tpu as pltpu
from jax.sharding import PartitionSpec as P

inv_temp = 20.0
f32 = jnp.float32
bf16 = jnp.bfloat16
AXES = ("pb", "pa")


def call(kernel, outs, flops, *args):
    return pl.pallas_call(
        kernel,
        out_shape=[jax.ShapeDtypeStruct(s, d) for s, d in outs],
        compiler_params=pltpu.CompilerParams(vmem_limit_bytes=40 * 1024 * 1024),
        cost_estimate=pl.CostEstimate(flops=flops, bytes_accessed=8 << 20, transcendentals=0),
    )(*args)


def split(x):
    hi = x.astype(bf16)
    return hi, (x - hi.astype(f32)).astype(bf16)


def mm(a, b, dims):
    return lax.dot_general(a, b, (dims, ((), ())), preferred_element_type=f32)


def mm3(a, b, dims):
    (ah, al), (bh, bl) = a, b
    return mm(al, bh, dims) + mm(ah, bl, dims) + mm(ah, bh, dims)


def normalize(rows):
    scale = lax.rsqrt(jnp.sum(rows * rows, axis=1, keepdims=True) + 1e-06)
    return rows * scale, scale


def onehot(pos, shape, first):
    return lax.broadcasted_iota(jnp.int32, shape, 0) + first == pos


def combine(stats):
    n = stats[0].shape[1] // len(stats)
    blocks = [sum(r[:, (m ^ k) * n : (m ^ k) * n + n] for k, r in enumerate(stats)) for m in range(len(stats))]
    return jnp.concatenate(blocks, axis=1)


def load(parts, hi, lo):
    at = 0
    for r in parts:
        n = r.shape[0]
        hi[at : at + n], lo[at : at + n] = split(normalize(r[...])[0])
        at += n


def product(p, q):
    return inv_temp * mm3((p[0][...], p[1][...]), (q[0][...], q[1][...]), ((1,), (1,)))


def first_scores_kernel(n_q, n_p, *refs):
    qs, ps = refs[:n_q], refs[n_q : n_q + n_p]
    pos, et, stats, qh, ql, ph, pl_ = refs[n_q + n_p :]
    load(qs, qh, ql)
    load(ps, ph, pl_)
    st = product((ph, pl_), (qh, ql))
    write_stats(stats, et, st, pos[:, : st.shape[1]], 0)


def write_stats(stats, et, st, pos, first):
    e = jnp.exp(st)
    et[...] = e
    stats[...] = jnp.zeros(stats.shape, f32)
    stats[0:1] = jnp.sum(e, axis=0, keepdims=True)
    stats[1:2] = jnp.sum(jnp.where(onehot(pos, st.shape, first), st, 0.0), axis=0, keepdims=True)


def rest_scores_kernel(n_q, n_p, *refs):
    qs, ps = refs[:n_q], refs[n_q : n_q + n_p]
    pos, et1, stats1, qh1, ql1, ph1, pl1, et, stats, qh, ql, ph, pl_ = refs[n_q + n_p :]
    n, m = qh1.shape[0], ph1.shape[0]
    rows, cols = qh.shape[0], m + ph.shape[0]
    qh[:n] = qh1[...]
    ql[:n] = ql1[...]
    load(qs, qh.at[n:], ql.at[n:])
    load(ps, ph, pl_)
    top = product((ph1, pl1), (qh.at[n:], ql.at[n:]))
    low = product((ph, pl_), (qh, ql))
    e_top, e_low = jnp.exp(top), jnp.exp(low)
    et[:m, :n] = et1[...]
    et[:m, n:] = e_top
    et[m:, :] = e_low
    o_top, o_low = onehot(pos[:, n:], top.shape, 0), onehot(pos[...], low.shape, m)
    sum_low = jnp.sum(e_low, axis=0, keepdims=True)
    pos_low = jnp.sum(jnp.where(o_low, low, 0.0), axis=0, keepdims=True)
    stats[...] = jnp.zeros(stats.shape, f32)
    stats[0:1, :n] = stats1[0:1] + sum_low[:, :n]
    stats[1:2, :n] = stats1[1:2] + pos_low[:, :n]
    stats[0:1, n:] = jnp.sum(e_top, axis=0, keepdims=True) + sum_low[:, n:]
    stats[1:2, n:] = jnp.sum(jnp.where(o_top, top, 0.0), axis=0, keepdims=True) + pos_low[:, n:]


def unscaled_kernel(n_p, et, pos, *refs):
    ps, (u, v) = refs[: 2 * n_p], refs[2 * n_p :]
    at = 0
    for ph, pl_ in zip(ps[:n_p], ps[n_p:]):
        n = ph.shape[0]
        p = (ph[...], pl_[...])
        o = onehot(pos[...], (n, et.shape[1]), at).astype(f32).T.astype(bf16)
        part_u = mm3(split(et[at : at + n].T), p, ((1,), (0,)))
        part_v = mm(o, p[1], ((1,), (0,))) + mm(o, p[0], ((1,), (0,)))
        u[...] = part_u if at == 0 else u[...] + part_u
        v[...] = part_v if at == 0 else v[...] + part_v
        at += n


def scale_kernel(n_stats, q_cuts, p_rows, *refs):
    stats = refs[:n_stats]
    u, v, et, pos, qh, ql, losses, dh, dl, *outs = refs[n_stats:]
    both = combine(stats)
    losses[...] = jnp.log(both[0:1]) - both[1:2]
    total = both[0:1]
    d = et[...] * (1.0 / total) - onehot(pos[...], et.shape, 0).astype(f32)
    dh[...], dl[...] = split(d)
    at = et.shape[0]
    q = (qh[...], ql[...])
    for out, n in reversed(list(zip(outs[len(q_cuts) :], p_rows))):
        at -= n
        out[...] = mm3((dh[at : at + n], dl[at : at + n]), q, ((1,), (0,)))
    inv = (1.0 / both).T[:, 0:1]
    at = u.shape[0]
    for out, n in reversed(list(zip(outs, q_cuts))):
        at -= n
        out[...] = u[at : at + n] * inv[at : at + n] - v[at : at + n]


def passage_kernel(cuts, dh, dl, qh, ql, *outs):
    q = (qh[...], ql[...])
    at = 0
    for out, n in zip(outs, cuts):
        out[...] = mm3((dh[at : at + n], dl[at : at + n]), q, ((1,), (0,)))
        at += n


def query_kernel(n_stats, *refs):
    stats = refs[:n_stats]
    u, v, fa, fb, gx, gy, own = refs[n_stats:]
    inv = (1.0 / combine(stats)).T[:, 0:1]
    h = fa.shape[0]

    def part(k):
        return u[k * h : k * h + h] * inv[k * h : k * h + h] - v[k * h : k * h + h]

    gx[:h] = part(2)
    gx[h:] = part(3) + fb[...]
    gy[:h] = part(4) + fa[...]
    gy[h:] = part(5)
    own[:h] = part(0)
    own[h:] = part(1)


def final_kernel(*refs):
    rows, parts, out = refs[0], refs[1:-1], refs[-1]
    xn, scale = normalize(rows[...])
    g = parts[0][...]
    for part in parts[1:]:
        g = g + part[...]
    g = inv_temp * g
    out[...] = scale * (g - xn * jnp.sum(xn * g, axis=1, keepdims=True))


def flip(x, mask, only=None):
    n = lax.axis_size("pb") * lax.axis_size("pa")
    pairs = [(i, i ^ mask) for i in range(n) if only is None or only(i)]
    return lax.ppermute(x, AXES, pairs)


X, Y, C, Z1, Z2, Z3 = 1, 2, 4, 8, 16, 24


def middle(i):
    return (i // 8) in (1, 2)


def ends(i):
    return not middle(i)


def rows_of(x, *cuts):
    at, out = 0, []
    for n in cuts:
        out.append(lax.slice_in_dim(x, at, at + n, axis=0))
        at += n
    return out


def after(x, *others):
    return lax.optimization_barrier((x,) + others)[0]


def small_body(queries, passages, positive):
    qr, pr = queries.shape[0], passages.shape[0]
    h = qr // 2
    p_rows = 8 * pr
    pa, pb = lax.axis_index("pa"), lax.axis_index("pb")

    order = jnp.arange(4, dtype=jnp.int32) ^ pa
    pos = positive.reshape(4, qr)[order].reshape(1, 4 * qr)
    block = ((pos % p_rows) // pr) ^ pb
    place = jnp.array([0, 3, 1, 4, 2, 5, 6, 7], jnp.int32)
    pos = jnp.where(pos // p_rows == pa, place[block] * pr + pos % pr, -1)

    x, y = flip(queries, X), flip(queries, Y)
    z2, z1 = flip(passages, Z2), flip(passages, Z1)
    c0 = flip(passages, C)
    da, db = flip(x[:h], Y), flip(y[h:], X)
    far = flip(z2, Z1, middle)
    mid = flip(after(passages, z2), Z3, middle)
    c1, c2 = flip(z1, C), flip(z2, C)
    first = first_scores([queries, x], [passages, z1, z2, c0], pos)
    z3 = mid + far
    c3 = flip(z3, C)

    et, stats, qh, ql, ph2, pl2 = rest_scores([y, da, db], [c1, c2, z3, c3], pos, first)
    et1, stats1, qh1, ql1, ph1, pl1 = first
    both = [stats, flip(stats, X), flip(stats, Y), flip(stats, X + Y)]
    u, v = unscaled(et, pos, [ph1, ph2], [pl1, pl2])
    losses, dh, dl, gda, gdb, g3, gc3 = scale(both, u, v, et, pos, qh, ql, (h, h), (pr, pr))

    t3 = flip(gc3, C)
    fa, fb = flip(gda, X), flip(gdb, Y)
    g3 = g3 + t3
    ff = flip(g3, Z1, ends)
    rmid = flip(g3, Z3, middle)
    gz, gc = passage_grads(dh, dl, qh, ql, (3 * pr, 3 * pr))
    tc = flip(gc, C)
    gx, gy, own = query_grads(both, u, v, fa, fb)
    rx, ry = flip(gx, X), flip(gy, Y)
    r1 = flip(after(gz[pr : 2 * pr] + tc[pr : 2 * pr], ff), Z1)
    r2 = flip(gz[2 * pr :] + tc[2 * pr :] + ff, Z2)

    losses = losses.reshape(4, qr)[order].reshape(4 * qr)
    query_grad = finish(queries, own, rx, ry)
    passage_grad = finish(passages, gz[:pr], tc[:pr], r1, rmid, r2)
    return losses, query_grad, passage_grad


def rows(parts):
    return sum(x.shape[0] for x in parts)


def first_scores(q_parts, p_parts, pos):
    q, p, d = rows(q_parts), rows(p_parts), q_parts[0].shape[1]
    return call(
        functools.partial(first_scores_kernel, len(q_parts), len(p_parts)),
        [((p, q), f32), ((8, q), f32), ((q, d), bf16), ((q, d), bf16), ((p, d), bf16), ((p, d), bf16)],
        6 * q * p * d,
        *q_parts,
        *p_parts,
        pos,
    )


def rest_scores(q_parts, p_parts, pos, first):
    p1, q1 = first[0].shape
    q, p, d = q1 + rows(q_parts), rows(p_parts), q_parts[0].shape[1]
    return call(
        functools.partial(rest_scores_kernel, len(q_parts), len(p_parts)),
        [((p1 + p, q), f32), ((8, q), f32), ((q, d), bf16), ((q, d), bf16), ((p, d), bf16), ((p, d), bf16)],
        6 * q * p * d,
        *q_parts,
        *p_parts,
        pos,
        *first,
    )


def unscaled(et, pos, hi, lo):
    p, q = et.shape
    d = hi[0].shape[1]
    return call(
        functools.partial(unscaled_kernel, len(hi)), [((q, d), f32)] * 2, 10 * q * p * d, et, pos, *hi, *lo
    )


def scale(both, u, v, et, pos, qh, ql, q_cuts, p_cuts):
    p, q = et.shape
    d = qh.shape[1]
    return call(
        functools.partial(scale_kernel, len(both), q_cuts, p_cuts),
        [((1, q), f32), ((p, q), bf16), ((p, q), bf16)] + [((n, d), f32) for n in q_cuts + p_cuts],
        6 * q * sum(p_cuts) * d,
        *both,
        u,
        v,
        et,
        pos,
        qh,
        ql,
    )


def passage_grads(dh, dl, qh, ql, cuts):
    q, d = qh.shape
    return call(
        functools.partial(passage_kernel, cuts), [((n, d), f32) for n in cuts], 6 * q * sum(cuts) * d, dh, dl, qh, ql
    )


def query_grads(both, u, v, fa, fb):
    h, d = fa.shape
    return call(
        functools.partial(query_kernel, len(both)), [((2 * h, d), f32)] * 3, 18 * h * d, *both, u, v, fa, fb
    )


def finish(rows, *parts):
    return call(final_kernel, [(rows.shape, f32)], 12 * rows.size, rows, *parts)[0]


def body(queries, passages, positive):
    pa = lax.axis_index("pa")
    q_full = lax.all_gather(queries, "pa", axis=0, tiled=True)
    p_full = lax.all_gather(passages, "pb", axis=0, tiled=True)
    p_rows, q_rows = p_full.shape[0], q_full.shape[0]
    pos = positive - pa * p_rows
    pos = jnp.where((pos >= 0) & (pos < p_rows), pos, -1).reshape(1, -1)
    et, stats, qh, ql, ph, pl_ = first_scores([q_full], [p_full], pos)
    both = [lax.psum(stats, "pa")]
    u, v = unscaled(et, pos, [ph], [pl_])
    losses, dh, dl, gq, gp = scale(both, u, v, et, pos, qh, ql, (q_rows,), (p_rows,))
    q_part = lax.psum_scatter(gq, "pa", scatter_dimension=0, tiled=True)
    p_part = lax.psum_scatter(gp, "pb", scatter_dimension=0, tiled=True)
    return losses.reshape(-1), finish(queries, q_part), finish(passages, p_part)


def solution(mesh):
    placed = (P(("pb", "pa"), None), P(("pa", "pb"), None), P("pb"))
    small = mesh.shape["pa"] == 4 and mesh.shape["pb"] == 8
    return jax.shard_map(
        small_body if small else body,
        mesh=mesh,
        in_specs=placed,
        out_specs=(P("pb"), P(("pb", "pa"), None), P(("pa", "pb"), None)),
        check_vma=False,
    )
```

```python
import functools

import jax
import jax.numpy as jnp
from jax import lax
from jax.experimental import pallas as pl
from jax.experimental.pallas import tpu as pltpu
from jax.sharding import PartitionSpec as P

inv_temp = 20.0
f32 = jnp.float32
bf16 = jnp.bfloat16
AXES = ("pb", "pa")


def call(kernel, outs, flops, *args, kept=True):
    return pl.pallas_call(
        kernel,
        out_shape=[pltpu.VMEM(s, d) if kept else jax.ShapeDtypeStruct(s, d) for s, d in outs],
        compiler_params=pltpu.CompilerParams(vmem_limit_bytes=24 * 1024 * 1024),
        cost_estimate=pl.CostEstimate(flops=flops, bytes_accessed=8 << 20, transcendentals=0),
    )(*args)


def split(x):
    hi = x.astype(bf16)
    return hi, (x - hi.astype(f32)).astype(bf16)


def mm(a, b, dims):
    return lax.dot_general(a, b, (dims, ((), ())), preferred_element_type=f32)


def mm3(a, b, dims):
    (ah, al), (bh, bl) = a, b
    n = ah.shape[0]
    if n > 256:
        return mm(al, bh, dims) + mm(ah, bl, dims) + mm(ah, bh, dims)
    both = mm(jnp.concatenate([al, ah], axis=0), bh, dims)
    return both[:n] + mm(ah, bl, dims) + both[n:]


def lift(scale):
    return jnp.broadcast_to(scale, (scale.shape[0], 128))


def normalize(rows):
    scale = lax.rsqrt(jnp.sum(rows * rows, axis=1, keepdims=True) + 1e-06)
    return rows * scale, scale


def onehot(pos, shape, first):
    return lax.broadcasted_iota(jnp.int32, shape, 0) + first == pos


def combine(stats):
    n = stats[0].shape[1] // len(stats)
    blocks = [sum(r[:, (m ^ k) * n : (m ^ k) * n + n] for k, r in enumerate(stats)) for m in range(len(stats))]
    return jnp.concatenate(blocks, axis=1)


def load(parts, hi, lo):
    at = 0
    for r in parts:
        if isinstance(r, tuple):
            n = r[0].shape[0]
            hi[at : at + n], lo[at : at + n] = r[0][...], r[1][...]
        else:
            n = r.shape[0]
            hi[at : at + n], lo[at : at + n] = split(normalize(r[...])[0])
        at += n


def own_kernel(queries, passages, qn, qs, qh, ql, pn, ps, ph, pl_):
    for rows, xn, scale, hi, lo in ((queries, qn, qs, qh, ql), (passages, pn, ps, ph, pl_)):
        x, r = normalize(rows[...])
        xn[...] = x
        scale[...] = lift(r)
        hi[...], lo[...] = split(x)


def product(p, q):
    return inv_temp * mm3((p[0][...], p[1][...]), (q[0][...], q[1][...]), ((1,), (1,)))


def positives(pos, ph, pl_, first):
    o = onehot(pos[...], (ph.shape[0], pos.shape[1]), first).astype(f32).T.astype(bf16)
    return mm(o, pl_[...], ((1,), (0,))) + mm(o, ph[...], ((1,), (0,)))


def first_scores_kernel(*refs):
    qh0, ql0, ph0, pl0, x, y, *ps, pos, et, stats, qh, ql, ph, pl_, v = refs
    load([(qh0, ql0), x, y], qh, ql)
    load([(ph0, pl0), *ps], ph, pl_)
    st = product((ph, pl_), (qh, ql))
    write_stats(stats, et, st, pos[:, : st.shape[1]], 0)
    v[...] = positives(pos, ph, pl_, 0)


def all_scores_kernel(q, p, pos, et, stats, qh, ql, ph, pl_):
    load([q], qh, ql)
    load([p], ph, pl_)
    write_stats(stats, et, product((ph, pl_), (qh, ql)), pos[...], 0)


def write_stats(stats, et, st, pos, first):
    e = jnp.exp(st)
    et[...] = e
    stats[...] = jnp.zeros(stats.shape, f32)
    stats[0:1] = jnp.sum(e, axis=0, keepdims=True)
    stats[1:2] = jnp.sum(jnp.where(onehot(pos, st.shape, first), st, 0.0), axis=0, keepdims=True)


def rest_scores_kernel(n_q, n_p, *refs):
    qs, ps = refs[:n_q], refs[n_q : n_q + n_p]
    pos, et1, stats1, qh1, ql1, ph1, pl1, v1, et, stats, qh, ql, ph, pl_ = refs[n_q + n_p :]
    n, m = qh1.shape[0], ph1.shape[0]
    del v1
    qh[:n] = qh1[...]
    ql[:n] = ql1[...]
    load(qs, qh.at[n:], ql.at[n:])
    load(ps, ph, pl_)
    top = product((ph1, pl1), (qh.at[n:], ql.at[n:]))
    low = product((ph, pl_), (qh, ql))
    e_top, e_low = jnp.exp(top), jnp.exp(low)
    et[:m, :n] = et1[...]
    et[:m, n:] = e_top
    et[m:, :] = e_low
    o_top, o_low = onehot(pos[:, n:], top.shape, 0), onehot(pos[...], low.shape, m)
    sum_low = jnp.sum(e_low, axis=0, keepdims=True)
    pos_low = jnp.sum(jnp.where(o_low, low, 0.0), axis=0, keepdims=True)
    stats[...] = jnp.zeros(stats.shape, f32)
    stats[0:1, :n] = stats1[0:1] + sum_low[:, :n]
    stats[1:2, :n] = stats1[1:2] + pos_low[:, :n]
    stats[0:1, n:] = jnp.sum(e_top, axis=0, keepdims=True) + sum_low[:, n:]
    stats[1:2, n:] = jnp.sum(jnp.where(o_top, top, 0.0), axis=0, keepdims=True) + pos_low[:, n:]


def unscaled_kernel(n_p, et, pos, *refs):
    ps, v1, (u, v) = refs[: 2 * n_p], refs[2 * n_p : -2], refs[-2:]
    at = 0
    for ph, pl_ in zip(ps[:n_p], ps[n_p:]):
        n = ph.shape[0]
        part_u = mm3(split(et[at : at + n].T), (ph[...], pl_[...]), ((1,), (0,)))
        u[...] = part_u if at == 0 else u[...] + part_u
        at += n
    v[...] = positives(pos, ph, pl_, at - n) + (v1[0][...] if v1 else 0.0)


def query_kernel(n_stats, cuts, *refs):
    stats = refs[:n_stats]
    u, v, losses, *outs = refs[n_stats:]
    both = combine(stats)
    losses[...] = jnp.log(both[0:1]) - both[1:2]
    inv = (1.0 / both).T[:, 0:1]
    for out, ranges in zip(outs, cuts):
        at = 0
        for a, b in ranges:
            out[at : at + b - a] = u[a:b] * inv[a:b] - v[a:b]
            at += b - a


def passage_kernel(n_stats, cuts, *refs):
    stats = refs[:n_stats]
    et, pos, qh, ql, *outs = refs[n_stats:]
    weight = 1.0 / combine(stats)[0:1]
    d = et[...] * weight - onehot(pos[...], et.shape, 0).astype(f32)
    g = mm3(split(d), (qh[...], ql[...]), ((1,), (0,)))
    at = 0
    for out, n in zip(outs, cuts):
        out[...] = g[at : at + n]
        at += n


def core_sum_kernel(g, tc, g3, t1, t2, t3):
    n = g3.shape[0]
    t1[...] = g[n : 2 * n] + tc[n : 2 * n]
    t2[...] = g[2 * n :] + tc[2 * n : 3 * n]
    t3[...] = g3[...] + tc[3 * n :]


def add_kernel(a, b, out):
    out[...] = a[...] + b[...]


def cross_kernel(gx, gy, x1, y1, x, y):
    n = gx.shape[0]
    h = (n + x1.shape[0]) // 3
    x[: n - h] = gx[: n - h]
    x[n - h :] = gx[n - h :] + y1[:h]
    y[:h] = gy[:h] + x1[:h]
    y[h:] = gy[h:]


def project(g, xn, scale):
    g = inv_temp * g
    return scale * (g - xn * jnp.sum(xn * g, axis=1, keepdims=True))


def last_kernel(qn, qs, pn, ps, own, x1, y1, x2, y2, g, tc, r1, rmid, r2, out_q, out_p):
    h, m = qn.shape[0] // 2, pn.shape[0]
    k = x1.shape[0] - h
    for at, n, p, pa, q, qa in ((0, k, x1, h, y2, 0), (k, h - k, x2, 0, y2, k), (h, k, y1, h, x2, h - k), (h + k, h - k, y2, h, x2, h)):
        if n:
            s = own[at : at + n] + p[pa : pa + n] + q[qa : qa + n]
            out_q[at : at + n] = project(s, qn[at : at + n], qs[at : at + n, 0:1])
    out_p[...] = project(g[:m] + tc[:m] + r1[...] + rmid[...] + r2[...], pn[...], ps[:, 0:1])


def final_kernel(rows, g, out):
    xn, scale = normalize(rows[...])
    out[...] = project(g[...], xn, scale)


def flip(x, mask, only=None):
    n = lax.axis_size("pb") * lax.axis_size("pa")
    pairs = [(i, i ^ mask) for i in range(n) if only is None or only(i)]
    return lax.ppermute(x, AXES, pairs)


X, Y, C, Z1, Z2, Z3 = 1, 2, 4, 8, 16, 24
EARLY = 2


def middle(i):
    return (i // 8) in (1, 2)


def ends(i):
    return not middle(i)


def rows_of(x, *cuts):
    at, out = 0, []
    for n in cuts:
        out.append(lax.slice_in_dim(x, at, at + n, axis=0))
        at += n
    return out


def after(x, *others):
    return lax.optimization_barrier((x,) + others)[0]


def by_xor(x, k):
    x = jnp.where(k & 1, jnp.stack([x[1], x[0], x[3], x[2]]), x)
    return jnp.where(k & 2, jnp.stack([x[2], x[3], x[0], x[1]]), x)


def small_body(queries, passages, positive):
    qr, pr = queries.shape[0], passages.shape[0]
    h = qr // 2
    p_rows = 8 * pr
    pa, pb = lax.axis_index("pa"), lax.axis_index("pb")

    pos = by_xor(positive.reshape(4, qr), pa).reshape(1, 4 * qr)
    block = ((pos % p_rows) // pr) ^ pb
    place = jnp.where(block == 6, 7, block // 2 + 3 * (block % 2))
    pos = jnp.where(pos // p_rows == pa, place * pr + pos % pr, -1)

    z2, z1 = flip(passages, Z2), flip(passages, Z1)
    x, y = flip(queries, X), flip(queries, Y)
    c0 = flip(passages, C)
    qn, qs, qh0, ql0, pn, ps, ph0, pl0 = own_rows(queries, passages)
    z2 = after(z2, qh0, pos)
    far = flip(z2, Z1, middle)
    mid = flip(after(passages, z2), Z3, middle)
    da, db = flip(after(x[:h], c0), Y), flip(after(y[h:], c0), X)
    c1 = flip(after(z1, qh0, pos), C)
    c2 = flip(after(z2, c1), C)
    first = first_scores((qh0, ql0, ph0, pl0, x, y, z1, z2, c0), pos)
    z3 = mid + far
    c3 = flip(z3, C)

    et, stats, qh, ql, ph2, pl2 = rest_scores([da, db], [c1, c2, c3, z3], pos, first)
    ph1, pl1, v1 = first[4:]
    both = [stats, flip(stats, X), flip(stats, Y), flip(stats, X + Y)]
    u, v = unscaled(et, pos, (ph1, ph2), (pl1, pl2), (v1,))

    def part(k, n):
        return (k * n, k * n + n)

    g, gc, g3 = passage_grads(both, after(et, u), pos, qh, ql, (3 * pr, 4 * pr, pr))
    tc = flip(gc, C)
    k = EARLY * h // 4
    kx, ky = 2 * h + k, 5 * h + k
    cuts = ((part(6, h), (2 * h, kx)), (part(7, h), (5 * h, ky)), ((kx, 4 * h),), (part(4, h), (ky, 6 * h)), ((0, qr),))
    losses, gx1, gy1, gx, gy, own = query_grads(both, after(u, gc), v, cuts)
    x1, y1 = flip(gx1, X), flip(gy1, Y)
    t1, t2, t3 = core_sums(g, tc, g3)
    ff = flip(t3, Z1, ends)
    rmid = flip(t3, Z3, middle)
    t2 = add(t2, ff)
    r1, r2 = flip(after(t1, t2, rmid), Z1), flip(t2, Z2)
    gx, gy = cross(after(gx, t2), gy, x1, y1)
    x2, y2 = flip(gx, X), flip(gy, Y)

    losses = by_xor(losses.reshape(4, qr), pa).reshape(4 * qr)
    query_grad, passage_grad = call(
        last_kernel,
        [(queries.shape, f32), (passages.shape, f32)],
        12 * queries.size,
        *(qn, qs, pn, ps, own, x1, y1, x2, y2, g, tc, r1, rmid, r2),
        kept=False,
    )
    return losses, query_grad, passage_grad


def rows(parts):
    return sum(x.shape[0] for x in parts)


def own_rows(queries, passages):
    outs = []
    for n, d in (queries.shape, passages.shape):
        outs += [((n, d), f32), ((n, 128), f32), ((n, d), bf16), ((n, d), bf16)]
    return call(own_kernel, outs, 4 * queries.size, queries, passages)


def scores_outs(q, p, d):
    return [((p, q), f32), ((8, q), f32), ((q, d), bf16), ((q, d), bf16), ((p, d), bf16), ((p, d), bf16)]


def first_scores(parts, pos):
    qh0, _, ph0, _, x, y, *ps = parts
    q, p, d = rows([qh0, x, y]), rows([ph0] + ps), x.shape[1]
    return call(
        first_scores_kernel, scores_outs(q, p, d) + [((pos.shape[1], d), f32)], 10 * q * p * d, *parts, pos
    )


def all_scores(q, p, pos):
    work = 6 * q.size * p.shape[0]
    return call(all_scores_kernel, scores_outs(q.shape[0], p.shape[0], q.shape[1]), work, q, p, pos)


def rest_scores(q_parts, p_parts, pos, first):
    p1, q1 = first[0].shape
    q, p, d = q1 + rows(q_parts), rows(p_parts), q_parts[0].shape[1]
    return call(
        functools.partial(rest_scores_kernel, len(q_parts), len(p_parts)),
        [((p1 + p, q), f32)] + scores_outs(q, p, d)[1:],
        6 * q * p * d,
        *q_parts,
        *p_parts,
        pos,
        *first,
    )


def unscaled(et, pos, hi, lo, v=()):
    p, q = et.shape
    d = hi[0].shape[1]
    kernel = functools.partial(unscaled_kernel, len(hi))
    return call(kernel, [((q, d), f32)] * 2, 8 * q * p * d, et, pos, *hi, *lo, *v)


def query_grads(both, u, v, cuts):
    q, d = u.shape
    return call(
        functools.partial(query_kernel, len(both), cuts),
        [((1, q), f32)] + [((sum(b - a for a, b in ranges), d), f32) for ranges in cuts],
        3 * q * d,
        *both,
        u,
        v,
    )


def passage_grads(both, et, pos, qh, ql, cuts):
    q, d = qh.shape
    return call(
        functools.partial(passage_kernel, len(both), cuts),
        [((n, d), f32) for n in cuts],
        6 * q * d * sum(cuts),
        *both,
        et,
        pos,
        qh,
        ql,
    )


def add(a, b):
    return call(add_kernel, [(a.shape, f32)], a.size, a, b)[0]


def core_sums(g, tc, g3):
    return call(core_sum_kernel, [(g3.shape, f32)] * 3, 3 * g3.size, g, tc, g3)


def cross(gx, gy, x1, y1):
    return call(cross_kernel, [(gx.shape, f32)] * 2, 2 * gx.size, gx, gy, x1, y1)


def finish(rows, g):
    return call(final_kernel, [(rows.shape, f32)], 12 * rows.size, rows, g, kept=False)[0]


def body(queries, passages, positive):
    pa = lax.axis_index("pa")
    q_full = lax.all_gather(queries, "pa", axis=0, tiled=True)
    p_full = lax.all_gather(passages, "pb", axis=0, tiled=True)
    p_rows, q_rows = p_full.shape[0], q_full.shape[0]
    pos = positive - pa * p_rows
    pos = jnp.where((pos >= 0) & (pos < p_rows), pos, -1).reshape(1, -1)
    et, stats, qh, ql, ph, pl_ = all_scores(q_full, p_full, pos)
    both = [lax.psum(stats, "pa")]
    u, v = unscaled(et, pos, [ph], [pl_])
    losses, gq = query_grads(both, u, v, (((0, q_rows),),))
    (gp,) = passage_grads(both, et, pos, qh, ql, (p_rows,))
    q_part = lax.psum_scatter(gq, "pa", scatter_dimension=0, tiled=True)
    p_part = lax.psum_scatter(gp, "pb", scatter_dimension=0, tiled=True)
    return losses.reshape(-1), finish(queries, q_part), finish(passages, p_part)


def solution(mesh):
    placed = (P(("pb", "pa"), None), P(("pa", "pb"), None), P("pb"))
    small = mesh.shape["pa"] == 4 and mesh.shape["pb"] == 8
    return jax.shard_map(
        small_body if small else body,
        mesh=mesh,
        in_specs=placed,
        out_specs=(P("pb"), P(("pb", "pa"), None), P(("pa", "pb"), None)),
        check_vma=False,
    )
```

```python
import functools

import jax
import jax.numpy as jnp
from jax import lax
from jax.experimental import pallas as pl
from jax.experimental.pallas import tpu as pltpu
from jax.sharding import PartitionSpec as P

inv_temp = 20.0
f32 = jnp.float32
bf16 = jnp.bfloat16
AXES = ("pb", "pa")


def call(kernel, outs, flops, *args, kept=True):
    return pl.pallas_call(
        kernel,
        out_shape=[pltpu.VMEM(s, d) if kept else jax.ShapeDtypeStruct(s, d) for s, d in outs],
        compiler_params=pltpu.CompilerParams(vmem_limit_bytes=24 * 1024 * 1024),
        cost_estimate=pl.CostEstimate(flops=flops, bytes_accessed=8 << 20, transcendentals=0),
    )(*args)


def split(x):
    hi = x.astype(bf16)
    return hi, (x - hi.astype(f32)).astype(bf16)


def mm(a, b, dims):
    return lax.dot_general(a, b, (dims, ((), ())), preferred_element_type=f32)


def mm3(a, b, dims):
    (ah, al), (bh, bl) = a, b
    n = ah.shape[0]
    if n > 256:
        return mm(al, bh, dims) + mm(ah, bl, dims) + mm(ah, bh, dims)
    both = mm(jnp.concatenate([al, ah], axis=0), bh, dims)
    return both[:n] + mm(ah, bl, dims) + both[n:]


def lift(scale):
    return jnp.broadcast_to(scale, (scale.shape[0], 128))


def normalize(rows):
    scale = lax.rsqrt(jnp.sum(rows * rows, axis=1, keepdims=True) + 1e-06)
    return rows * scale, scale


def onehot(pos, shape, first):
    return lax.broadcasted_iota(jnp.int32, shape, 0) + first == pos


def combine(stats):
    n = stats[0].shape[1] // len(stats)
    blocks = [sum(r[:, (m ^ k) * n : (m ^ k) * n + n] for k, r in enumerate(stats)) for m in range(len(stats))]
    return jnp.concatenate(blocks, axis=1)


def load(parts, hi, lo):
    at = 0
    for r in parts:
        if isinstance(r, tuple):
            n = r[0].shape[0]
            hi[at : at + n], lo[at : at + n] = r[0][...], r[1][...]
        else:
            n = r.shape[0]
            hi[at : at + n], lo[at : at + n] = split(normalize(r[...])[0])
        at += n


def own_kernel(queries, passages, qn, qs, qh, ql, pn, ps, ph, pl_):
    for rows, xn, scale, hi, lo in ((queries, qn, qs, qh, ql), (passages, pn, ps, ph, pl_)):
        x, r = normalize(rows[...])
        xn[...] = x
        scale[...] = lift(r)
        hi[...], lo[...] = split(x)


def product(p, q):
    return inv_temp * mm3((p[0][...], p[1][...]), (q[0][...], q[1][...]), ((1,), (1,)))


def positives(pos, ph, pl_, first):
    o = onehot(pos[...], (ph.shape[0], pos.shape[1]), first).astype(f32).T.astype(bf16)
    return mm(o, pl_[...], ((1,), (0,))) + mm(o, ph[...], ((1,), (0,)))


def first_scores_kernel(*refs):
    qh0, ql0, ph0, pl0, x, y, *ps, pos, et, stats, qh, ql, ph, pl_, v = refs
    load([(qh0, ql0), x, y], qh, ql)
    load([(ph0, pl0), *ps], ph, pl_)
    st = product((ph, pl_), (qh, ql))
    write_stats(stats, et, st, pos[:, : st.shape[1]], 0)
    v[...] = positives(pos, ph, pl_, 0)


def all_scores_kernel(q, p, pos, et, stats, qh, ql, ph, pl_):
    load([q], qh, ql)
    load([p], ph, pl_)
    write_stats(stats, et, product((ph, pl_), (qh, ql)), pos[...], 0)


def write_stats(stats, et, st, pos, first):
    e = jnp.exp(st)
    et[...] = e
    stats[...] = jnp.zeros(stats.shape, f32)
    stats[0:1] = jnp.sum(e, axis=0, keepdims=True)
    stats[1:2] = jnp.sum(jnp.where(onehot(pos, st.shape, first), st, 0.0), axis=0, keepdims=True)


def rest_scores_kernel(n_q, n_p, *refs):
    qs, ps = refs[:n_q], refs[n_q : n_q + n_p]
    pos, et1, stats1, qh1, ql1, ph1, pl1, v1, et, stats, qh, ql, ph, pl_ = refs[n_q + n_p :]
    n, m = qh1.shape[0], ph1.shape[0]
    del v1
    qh[:n] = qh1[...]
    ql[:n] = ql1[...]
    load(qs, qh.at[n:], ql.at[n:])
    load(ps, ph, pl_)
    top = product((ph1, pl1), (qh.at[n:], ql.at[n:]))
    low = product((ph, pl_), (qh, ql))
    e_top, e_low = jnp.exp(top), jnp.exp(low)
    et[:m, :n] = et1[...]
    et[:m, n:] = e_top
    et[m:, :] = e_low
    o_top, o_low = onehot(pos[:, n:], top.shape, 0), onehot(pos[...], low.shape, m)
    sum_low = jnp.sum(e_low, axis=0, keepdims=True)
    pos_low = jnp.sum(jnp.where(o_low, low, 0.0), axis=0, keepdims=True)
    stats[...] = jnp.zeros(stats.shape, f32)
    stats[0:1, :n] = stats1[0:1] + sum_low[:, :n]
    stats[1:2, :n] = stats1[1:2] + pos_low[:, :n]
    stats[0:1, n:] = jnp.sum(e_top, axis=0, keepdims=True) + sum_low[:, n:]
    stats[1:2, n:] = jnp.sum(jnp.where(o_top, top, 0.0), axis=0, keepdims=True) + pos_low[:, n:]


def unscaled_kernel(n_p, et, pos, *refs):
    ps, v1, (u, v) = refs[: 2 * n_p], refs[2 * n_p : -2], refs[-2:]
    at = 0
    for ph, pl_ in zip(ps[:n_p], ps[n_p:]):
        n = ph.shape[0]
        part_u = mm3(split(et[at : at + n].T), (ph[...], pl_[...]), ((1,), (0,)))
        u[...] = part_u if at == 0 else u[...] + part_u
        at += n
    v[...] = positives(pos, ph, pl_, at - n) + (v1[0][...] if v1 else 0.0)


def query_kernel(n_stats, cuts, *refs):
    stats = refs[:n_stats]
    u, v, losses, *outs = refs[n_stats:]
    both = combine(stats)
    losses[...] = jnp.log(both[0:1]) - both[1:2]
    inv = (1.0 / both).T[:, 0:1]
    for out, ranges in zip(outs, cuts):
        at = 0
        for a, b in ranges:
            out[at : at + b - a] = u[a:b] * inv[a:b] - v[a:b]
            at += b - a


def passage_kernel(n_stats, cuts, *refs):
    stats = refs[:n_stats]
    et, pos, qh, ql, *outs = refs[n_stats:]
    weight = 1.0 / combine(stats)[0:1]
    d = [et[a:b] * weight - onehot(pos[...], (b - a, et.shape[1]), a).astype(f32) for a, b in cuts]
    g = mm3(split(jnp.concatenate(d, axis=0)), (qh[...], ql[...]), ((1,), (0,)))
    at = 0
    for out, (a, b) in zip(outs, cuts):
        out[...] = g[at : at + b - a]
        at += b - a


def core_sum_kernel(g, tc, g3, t1, t2, t3):
    n = g3.shape[0]
    t1[...] = g[n : 2 * n] + tc[n : 2 * n]
    t2[...] = g[2 * n :] + tc[2 * n : 3 * n]
    t3[...] = g3[...] + tc[3 * n :]


def add_kernel(a, b, out):
    out[...] = a[...] + b[...]


def cross_kernel(gx, gy, x1, y1, x, y):
    n = gx.shape[0]
    h = (n + x1.shape[0]) // 3
    x[: n - h] = gx[: n - h]
    x[n - h :] = gx[n - h :] + y1[:h]
    y[:h] = gy[:h] + x1[:h]
    y[h:] = gy[h:]


def project(g, xn, scale):
    g = inv_temp * g
    return scale * (g - xn * jnp.sum(xn * g, axis=1, keepdims=True))


def last_kernel(qn, qs, pn, ps, own, x1, y1, x2, y2, g, tc, r1, r2, out_q, out_p):
    h, m = qn.shape[0] // 2, pn.shape[0]
    k = x1.shape[0] - h
    for at, n, p, pa, q, qa in ((0, k, x1, h, y2, 0), (k, h - k, x2, 0, y2, k), (h, k, y1, h, x2, h - k), (h + k, h - k, y2, h, x2, h)):
        if n:
            s = own[at : at + n] + p[pa : pa + n] + q[qa : qa + n]
            out_q[at : at + n] = project(s, qn[at : at + n], qs[at : at + n, 0:1])
    out_p[...] = project(g[:m] + tc[:m] + r1[...] + r2[...], pn[...], ps[:, 0:1])


def final_kernel(rows, g, out):
    xn, scale = normalize(rows[...])
    out[...] = project(g[...], xn, scale)


def flip(x, mask):
    n = lax.axis_size("pb") * lax.axis_size("pa")
    return lax.ppermute(x, AXES, [(i, i ^ mask) for i in range(n)])


X, Y, C, Z1, Z2 = 1, 2, 4, 8, 16
EARLY = 2


def after(x, *others):
    return lax.optimization_barrier((x,) + others)[0]


def by_xor(x, k):
    x = jnp.where(k & 1, jnp.stack([x[1], x[0], x[3], x[2]]), x)
    return jnp.where(k & 2, jnp.stack([x[2], x[3], x[0], x[1]]), x)


def small_body(queries, passages, positive):
    qr, pr = queries.shape[0], passages.shape[0]
    h = qr // 2
    p_rows = 8 * pr
    pa, pb = lax.axis_index("pa"), lax.axis_index("pb")

    pos = by_xor(positive.reshape(4, qr), pa).reshape(1, 4 * qr)
    block = ((pos % p_rows) // pr) ^ pb
    place = jnp.where(block == 6, 7, block // 2 + 3 * (block % 2))
    pos = jnp.where(pos // p_rows == pa, place * pr + pos % pr, -1)

    z2, z1 = flip(passages, Z2), flip(passages, Z1)
    x, y = flip(queries, X), flip(queries, Y)
    c0 = flip(passages, C)
    qn, qs, qh0, ql0, pn, ps, ph0, pl0 = own_rows(queries, passages)
    z2 = after(z2, qh0, pos)
    z3 = flip(z2, Z1)
    da, db = flip(after(x[:h], c0), Y), flip(after(y[h:], c0), X)
    c1 = flip(after(z1, qh0, pos), C)
    c2 = flip(after(z2, c1), C)
    first = first_scores((qh0, ql0, ph0, pl0, x, y, z1, z2, c0), pos)
    c3 = flip(z3, C)

    et, stats, qh, ql, ph2, pl2 = rest_scores([da, db], [c1, c2, c3, z3], pos, first)
    ph1, pl1, v1 = first[4:]
    both = [stats, flip(stats, X), flip(stats, Y), flip(stats, X + Y)]
    u, v = unscaled(et, pos, (ph1, ph2), (pl1, pl2), (v1,))

    def part(k, n):
        return (k * n, k * n + n)

    (gc,) = passage_grads(both, after(et, u), pos, qh, ql, ((3 * pr, 7 * pr),))
    tc = flip(gc, C)
    g, g3 = passage_grads(both, after(et, gc), pos, qh, ql, ((0, 3 * pr), (7 * pr, 8 * pr)))
    k = EARLY * h // 4
    kx, ky = 2 * h + k, 5 * h + k
    cuts = ((part(6, h), (2 * h, kx)), (part(7, h), (5 * h, ky)), ((kx, 4 * h),), (part(4, h), (ky, 6 * h)), ((0, qr),))
    losses, gx1, gy1, gx, gy, own = query_grads(both, after(u, g), v, cuts)
    x1, y1 = flip(gx1, X), flip(gy1, Y)
    t1, t2, t3 = core_sums(g, tc, g3)
    r3 = flip(t3, Z1)
    t2 = add(t2, r3)
    r1, r2 = flip(after(t1, t2), Z1), flip(t2, Z2)
    gx, gy = cross(after(gx, t2), gy, x1, y1)
    x2, y2 = flip(gx, X), flip(gy, Y)

    losses = by_xor(losses.reshape(4, qr), pa).reshape(4 * qr)
    query_grad, passage_grad = call(
        last_kernel,
        [(queries.shape, f32), (passages.shape, f32)],
        12 * queries.size,
        *(qn, qs, pn, ps, own, x1, y1, x2, y2, g, tc, r1, r2),
        kept=False,
    )
    return losses, query_grad, passage_grad


def rows(parts):
    return sum(x.shape[0] for x in parts)


def own_rows(queries, passages):
    outs = []
    for n, d in (queries.shape, passages.shape):
        outs += [((n, d), f32), ((n, 128), f32), ((n, d), bf16), ((n, d), bf16)]
    return call(own_kernel, outs, 4 * queries.size, queries, passages)


def scores_outs(q, p, d):
    return [((p, q), f32), ((8, q), f32), ((q, d), bf16), ((q, d), bf16), ((p, d), bf16), ((p, d), bf16)]


def first_scores(parts, pos):
    qh0, _, ph0, _, x, y, *ps = parts
    q, p, d = rows([qh0, x, y]), rows([ph0] + ps), x.shape[1]
    return call(
        first_scores_kernel, scores_outs(q, p, d) + [((pos.shape[1], d), f32)], 10 * q * p * d, *parts, pos
    )


def all_scores(q, p, pos):
    work = 6 * q.size * p.shape[0]
    return call(all_scores_kernel, scores_outs(q.shape[0], p.shape[0], q.shape[1]), work, q, p, pos)


def rest_scores(q_parts, p_parts, pos, first):
    p1, q1 = first[0].shape
    q, p, d = q1 + rows(q_parts), rows(p_parts), q_parts[0].shape[1]
    return call(
        functools.partial(rest_scores_kernel, len(q_parts), len(p_parts)),
        [((p1 + p, q), f32)] + scores_outs(q, p, d)[1:],
        6 * q * p * d,
        *q_parts,
        *p_parts,
        pos,
        *first,
    )


def unscaled(et, pos, hi, lo, v=()):
    p, q = et.shape
    d = hi[0].shape[1]
    kernel = functools.partial(unscaled_kernel, len(hi))
    return call(kernel, [((q, d), f32)] * 2, 8 * q * p * d, et, pos, *hi, *lo, *v)


def query_grads(both, u, v, cuts):
    q, d = u.shape
    return call(
        functools.partial(query_kernel, len(both), cuts),
        [((1, q), f32)] + [((sum(b - a for a, b in ranges), d), f32) for ranges in cuts],
        3 * q * d,
        *both,
        u,
        v,
    )


def passage_grads(both, et, pos, qh, ql, cuts):
    q, d = qh.shape
    return call(
        functools.partial(passage_kernel, len(both), cuts),
        [((b - a, d), f32) for a, b in cuts],
        6 * q * d * sum(b - a for a, b in cuts),
        *both,
        et,
        pos,
        qh,
        ql,
    )


def add(a, b):
    return call(add_kernel, [(a.shape, f32)], a.size, a, b)[0]


def core_sums(g, tc, g3):
    return call(core_sum_kernel, [(g3.shape, f32)] * 3, 3 * g3.size, g, tc, g3)


def cross(gx, gy, x1, y1):
    return call(cross_kernel, [(gx.shape, f32)] * 2, 2 * gx.size, gx, gy, x1, y1)


def finish(rows, g):
    return call(final_kernel, [(rows.shape, f32)], 12 * rows.size, rows, g, kept=False)[0]


def body(queries, passages, positive):
    pa = lax.axis_index("pa")
    q_full = lax.all_gather(queries, "pa", axis=0, tiled=True)
    p_full = lax.all_gather(passages, "pb", axis=0, tiled=True)
    p_rows, q_rows = p_full.shape[0], q_full.shape[0]
    pos = positive - pa * p_rows
    pos = jnp.where((pos >= 0) & (pos < p_rows), pos, -1).reshape(1, -1)
    et, stats, qh, ql, ph, pl_ = all_scores(q_full, p_full, pos)
    both = [lax.psum(stats, "pa")]
    u, v = unscaled(et, pos, [ph], [pl_])
    losses, gq = query_grads(both, u, v, (((0, q_rows),),))
    (gp,) = passage_grads(both, et, pos, qh, ql, ((0, p_rows),))
    q_part = lax.psum_scatter(gq, "pa", scatter_dimension=0, tiled=True)
    p_part = lax.psum_scatter(gp, "pb", scatter_dimension=0, tiled=True)
    return losses.reshape(-1), finish(queries, q_part), finish(passages, p_part)


def solution(mesh):
    placed = (P(("pb", "pa"), None), P(("pa", "pb"), None), P("pb"))
    small = mesh.shape["pa"] == 4 and mesh.shape["pb"] == 8
    return jax.shard_map(
        small_body if small else body,
        mesh=mesh,
        in_specs=placed,
        out_specs=(P("pb"), P(("pb", "pa"), None), P(("pa", "pb"), None)),
        check_vma=False,
    )
```

```python
import functools

import jax
import jax.numpy as jnp
from jax import lax
from jax.experimental import pallas as pl
from jax.experimental.pallas import tpu as pltpu
from jax.sharding import PartitionSpec as P

inv_temp = 20.0
f32 = jnp.float32
bf16 = jnp.bfloat16
AXES = ("pb", "pa")
X, Y, C, Z1, Z2 = 1, 2, 4, 8, 16
EARLY = 2


def call(kernel, outs, flops, *args, kept=True):
    return pl.pallas_call(
        kernel,
        out_shape=[pltpu.VMEM(s, d) if kept else jax.ShapeDtypeStruct(s, d) for s, d in outs],
        compiler_params=pltpu.CompilerParams(vmem_limit_bytes=24 * 1024 * 1024),
        cost_estimate=pl.CostEstimate(flops=flops, bytes_accessed=8 << 20, transcendentals=0),
    )(*args)


def split(x):
    hi = x.astype(bf16)
    return hi, (x - hi.astype(f32)).astype(bf16)


def mm(a, b, dims):
    return lax.dot_general(a, b, (dims, ((), ())), preferred_element_type=f32)


def mm3(a, b, dims):
    (ah, al), (bh, bl) = a, b
    n = ah.shape[0]
    if n > 256:
        return mm(al, bh, dims) + mm(ah, bl, dims) + mm(ah, bh, dims)
    both = mm(jnp.concatenate([al, ah], axis=0), bh, dims)
    return both[:n] + mm(ah, bl, dims) + both[n:]


def lift(scale):
    return jnp.broadcast_to(scale, (scale.shape[0], 128))


def normalize(rows):
    scale = lax.rsqrt(jnp.sum(rows * rows, axis=1, keepdims=True) + 1e-06)
    return rows * scale, scale


def onehot(pos, shape, first):
    return lax.broadcasted_iota(jnp.int32, shape, 0) + first == pos


def combine(stats):
    n = stats[0].shape[1] // len(stats)
    blocks = [sum(r[:, (m ^ k) * n : (m ^ k) * n + n] for k, r in enumerate(stats)) for m in range(len(stats))]
    return jnp.concatenate(blocks, axis=1)


def load(parts, hi, lo):
    at = 0
    for r in parts:
        if isinstance(r, tuple):
            n = r[0].shape[0]
            hi[at : at + n], lo[at : at + n] = r[0][...], r[1][...]
        else:
            n = r.shape[0]
            hi[at : at + n], lo[at : at + n] = split(normalize(r[...])[0])
        at += n


def own_kernel(queries, passages, qn, qs, qh, ql, pn, ps, ph, pl_):
    for rows, xn, scale, hi, lo in ((queries, qn, qs, qh, ql), (passages, pn, ps, ph, pl_)):
        x, r = normalize(rows[...])
        xn[...] = x
        scale[...] = lift(r)
        hi[...], lo[...] = split(x)


def product(p, q):
    return inv_temp * mm3((p[0][...], p[1][...]), (q[0][...], q[1][...]), ((1,), (1,)))


def positives(pos, ph, pl_, first):
    o = onehot(pos[...], (ph.shape[0], pos.shape[1]), first).astype(f32).T.astype(bf16)
    return mm(o, pl_[...], ((1,), (0,))) + mm(o, ph[...], ((1,), (0,)))


def write_scores(et, stats, p, q, pos, first, new=False):
    st = product(p, q)
    e = jnp.exp(st)
    et[...] = e
    total = jnp.sum(e, axis=0, keepdims=True)
    spos = jnp.sum(jnp.where(onehot(pos, st.shape, first), st, 0.0), axis=0, keepdims=True)
    if new:
        stats[...] = jnp.zeros(stats.shape, f32)
        stats[0:1], stats[1:2] = total, spos
    else:
        stats[0:1] += total
        stats[1:2] += spos


def first_scores_kernel(*refs):
    qh0, ql0, ph0, pl0, x, y, z1, z2, c0, c1, c2, pos, et, stats, qh, ql, ph1, pl1, ph2, pl2, v = refs
    load([(qh0, ql0), x, y], qh, ql)
    load([(ph0, pl0), z1, z2, c0], ph1, pl1)
    load([c1, c2], ph2, pl2)
    m = ph1.shape[0]
    write_scores(et.at[:m], stats, (ph1, pl1), (qh, ql), pos[:, : et.shape[1]], 0, True)
    write_scores(et.at[m:], stats, (ph2, pl2), (qh, ql), pos[:, : et.shape[1]], m)
    v[...] = positives(pos, ph1, pl1, 0)


def rest_scores_kernel(da, db, c3, z3, pos, et1, stats1, qh1, ql1, ph1, pl1, phc, plc, et, stats, qh, ql, ph2, pl2):
    n, m, k, r = qh1.shape[0], ph1.shape[0], phc.shape[0], et1.shape[0]
    qh[:n], ql[:n] = qh1[...], ql1[...]
    ph2[:k], pl2[:k] = phc[...], plc[...]
    load([da, db], qh.at[n:], ql.at[n:])
    load([c3, z3], ph2.at[k:], pl2.at[k:])
    et[:r, :n] = et1[...]
    stats[:, :n] = stats1[...]
    last = (qh.at[n:], ql.at[n:])
    write_scores(et.at[:m, n:], stats.at[:, n:], (ph1, pl1), last, pos[:, n:], 0, True)
    write_scores(et.at[m:r, n:], stats.at[:, n:], (phc, plc), last, pos[:, n:], m)
    write_scores(et.at[r:], stats, (ph2.at[k:], pl2.at[k:]), (qh, ql), pos[...], r)


def all_scores_kernel(q, p, pos, et, stats, qh, ql, ph, pl_):
    load([q], qh, ql)
    load([p], ph, pl_)
    write_scores(et, stats, (ph, pl_), (qh, ql), pos[...], 0, True)


def others(et, pos, first, n):
    rows = et[first : first + n]
    return split(jnp.where(onehot(pos[...], rows.shape, first), 0.0, rows).T)


def unscaled_kernel(n_p, et, pos, *refs):
    ps, v1, (u, v) = refs[: 2 * n_p], refs[2 * n_p : -2], refs[-2:]
    at = 0
    for ph, pl_ in zip(ps[:n_p], ps[n_p:]):
        n = ph.shape[0]
        part_u = mm3(others(et, pos, at, n), (ph[...], pl_[...]), ((1,), (0,)))
        u[...] = part_u if at == 0 else u[...] + part_u
        at += n
    v[...] = positives(pos, ph, pl_, at - n) + (v1[0][...] if v1 else 0.0)


def query_kernel(n_stats, cuts, *refs):
    stats = refs[:n_stats]
    u, v, losses, *outs = refs[n_stats:]
    both = combine(stats)
    total, spos = both[0:1], both[1:2]
    losses[...] = jnp.log(total) - spos
    weight = 1.0 / total
    scales = jnp.concatenate([weight, jnp.exp(spos) * weight - 1.0, both[2:]], axis=0).T
    for out, ranges in zip(outs, cuts):
        at = 0
        for a, b in ranges:
            out[at : at + b - a] = u[a:b] * scales[a:b, 0:1] + v[a:b] * scales[a:b, 1:2]
            at += b - a


def passage_kernel(n_stats, cuts, *refs):
    stats = refs[:n_stats]
    et, pos, qh, ql, *outs = refs[n_stats:]
    weight = 1.0 / combine(stats)[0:1]
    d = [et[a:b] * weight - onehot(pos[...], (b - a, et.shape[1]), a).astype(f32) for a, b in cuts]
    g = mm3(split(jnp.concatenate(d, axis=0)), (qh[...], ql[...]), ((1,), (0,)))
    at = 0
    for out, (a, b) in zip(outs, cuts):
        out[...] = g[at : at + b - a]
        at += b - a


def core_sum_kernel(g, tc, g3, t1, t2, t3):
    n = g3.shape[0]
    t1[...] = g[n : 2 * n] + tc[n : 2 * n]
    t2[...] = g[2 * n :] + tc[2 * n : 3 * n]
    t3[...] = g3[...] + tc[3 * n :]


def add_kernel(a, b, out):
    out[...] = a[...] + b[...]


def cross_kernel(gx, gy, x1, y1, x, y):
    n = gx.shape[0]
    h = (n + x1.shape[0]) // 3
    x[: n - h] = gx[: n - h]
    x[n - h :] = gx[n - h :] + y1[:h]
    y[:h] = gy[:h] + x1[:h]
    y[h:] = gy[h:]


def project(g, xn, scale):
    g = inv_temp * g
    return scale * (g - xn * jnp.sum(xn * g, axis=1, keepdims=True))


def last_kernel(qn, qs, pn, ps, own, x1, y1, x2, y2, g, tc, r1, r2, out_q, out_p):
    h, m = qn.shape[0] // 2, pn.shape[0]
    k = x1.shape[0] - h
    for at, n, p, pa, q, qa in ((0, k, x1, h, y2, 0), (k, h - k, x2, 0, y2, k), (h, k, y1, h, x2, h - k), (h + k, h - k, y2, h, x2, h)):
        if n:
            s = own[at : at + n] + p[pa : pa + n] + q[qa : qa + n]
            out_q[at : at + n] = project(s, qn[at : at + n], qs[at : at + n, 0:1])
    out_p[...] = project(g[:m] + tc[:m] + r1[...] + r2[...], pn[...], ps[:, 0:1])


def final_kernel(rows, g, out):
    xn, scale = normalize(rows[...])
    out[...] = project(g[...], xn, scale)


def flip(x, mask):
    n = lax.axis_size("pb") * lax.axis_size("pa")
    return lax.ppermute(x, AXES, [(i, i ^ mask) for i in range(n)])


def after(x, *others):
    return lax.optimization_barrier((x,) + others)[0]


def by_xor(x, k):
    x = jnp.where(k & 1, jnp.stack([x[1], x[0], x[3], x[2]]), x)
    return jnp.where(k & 2, jnp.stack([x[2], x[3], x[0], x[1]]), x)


def small_body(queries, passages, positive):
    qr, pr = queries.shape[0], passages.shape[0]
    h = qr // 2
    p_rows = 8 * pr
    pa, pb = lax.axis_index("pa"), lax.axis_index("pb")

    pos = by_xor(positive.reshape(4, qr), pa).reshape(1, 4 * qr)
    block = ((pos % p_rows) // pr) ^ pb
    place = jnp.where(block == 6, 7, block // 2 + 3 * (block % 2))
    pos = jnp.where(pos // p_rows == pa, place * pr + pos % pr, -1)

    z2, z1 = flip(passages, Z2), flip(passages, Z1)
    x, y = flip(queries, X), flip(queries, Y)
    c0 = flip(passages, C)
    qn, qs, qh0, ql0, pn, ps, ph0, pl0 = own_rows(queries, passages)
    z2 = after(z2, qh0, pos)
    z3 = flip(z2, Z1)
    da, db = flip(after(x[:h], c0), Y), flip(after(y[h:], c0), X)
    c1 = flip(after(z1, qh0, pos), C)
    c2 = flip(after(z2, c1), C)
    *first, v1 = first_scores(qh0, ql0, ph0, pl0, x, y, z1, z2, c0, c1, c2, pos)
    c3 = flip(z3, C)
    et, stats, qh, ql, ph2, pl2 = rest_scores(da, db, c3, z3, pos, *first)
    ph1, pl1 = first[4:6]

    both = [stats, flip(stats, X), flip(stats, Y), flip(stats, X + Y)]
    u, v = unscaled(et, pos, (ph1, ph2), (pl1, pl2), (v1,))

    def part(k, n):
        return (k * n, k * n + n)

    (gc,) = passage_grads(both, after(et, u), pos, qh, ql, ((3 * pr, 7 * pr),))
    tc = flip(gc, C)
    g, g3 = passage_grads(both, after(et, gc), pos, qh, ql, ((0, 3 * pr), (7 * pr, 8 * pr)))
    k = EARLY * h // 4
    kx, ky = 2 * h + k, 5 * h + k
    cuts = ((part(6, h), (2 * h, kx)), (part(7, h), (5 * h, ky)), ((kx, 4 * h),), (part(4, h), (ky, 6 * h)), ((0, qr),))
    losses, gx1, gy1, gx, gy, own = query_grads(both, after(u, g), v, cuts)
    x1, y1 = flip(gx1, X), flip(gy1, Y)
    t1, t2, t3 = core_sums(g, tc, g3)
    r3 = flip(t3, Z1)
    t2 = add(t2, r3)
    r1, r2 = flip(after(t1, t2), Z1), flip(t2, Z2)
    gx, gy = cross(after(gx, t2), gy, x1, y1)
    x2, y2 = flip(gx, X), flip(gy, Y)

    losses = by_xor(losses.reshape(4, qr), pa).reshape(4 * qr)
    query_grad, passage_grad = call(
        last_kernel,
        [(queries.shape, f32), (passages.shape, f32)],
        12 * queries.size,
        *(qn, qs, pn, ps, own, x1, y1, x2, y2, g, tc, r1, r2),
        kept=False,
    )
    return losses, query_grad, passage_grad


def rows(parts):
    return sum(x.shape[0] for x in parts)


def own_rows(queries, passages):
    outs = []
    for n, d in (queries.shape, passages.shape):
        outs += [((n, d), f32), ((n, 128), f32), ((n, d), bf16), ((n, d), bf16)]
    return call(own_kernel, outs, 4 * queries.size, queries, passages)


def scores_outs(q, p, d):
    return [((p, q), f32), ((8, q), f32), ((q, d), bf16), ((q, d), bf16), ((p, d), bf16), ((p, d), bf16)]


def first_scores(qh0, ql0, ph0, pl0, x, y, z1, z2, c0, c1, c2, pos):
    q, p, d = rows([qh0, x, y]), rows([ph0, z1, z2, c0]), x.shape[1]
    k = rows([c1, c2])
    outs = [((p + k, q), f32), ((8, q), f32)] + [((n, d), bf16) for n in (q, q, p, p, k, k)] + [((pos.shape[1], d), f32)]
    return call(first_scores_kernel, outs, 10 * q * p * d, qh0, ql0, ph0, pl0, x, y, z1, z2, c0, c1, c2, pos)


def rest_scores(da, db, c3, z3, pos, et1, stats1, qh1, ql1, ph1, pl1, phc, plc):
    q, p, d = rows([qh1, da, db]), rows([phc, c3, z3]), da.shape[1]
    outs = [((rows([ph1]) + p, q), f32), ((8, q), f32)] + [((n, d), bf16) for n in (q, q, p, p)]
    args = (da, db, c3, z3, pos, et1, stats1, qh1, ql1, ph1, pl1, phc, plc)
    return call(rest_scores_kernel, outs, 6 * q * p * d, *args)


def all_scores(q, p, pos):
    work = 6 * q.size * p.shape[0]
    return call(all_scores_kernel, scores_outs(q.shape[0], p.shape[0], q.shape[1]), work, q, p, pos)


def unscaled(et, pos, hi, lo, v=()):
    p, q = et.shape
    d = hi[0].shape[1]
    kernel = functools.partial(unscaled_kernel, len(hi))
    return call(kernel, [((q, d), f32)] * 2, 8 * q * p * d, et, pos, *hi, *lo, *v)


def query_grads(both, u, v, cuts):
    q, d = u.shape
    return call(
        functools.partial(query_kernel, len(both), cuts),
        [((1, q), f32)] + [((sum(b - a for a, b in ranges), d), f32) for ranges in cuts],
        3 * q * d,
        *both,
        u,
        v,
    )


def passage_grads(both, et, pos, qh, ql, cuts):
    q, d = qh.shape
    return call(
        functools.partial(passage_kernel, len(both), cuts),
        [((b - a, d), f32) for a, b in cuts],
        6 * q * d * sum(b - a for a, b in cuts),
        *both,
        et,
        pos,
        qh,
        ql,
    )


def add(a, b):
    return call(add_kernel, [(a.shape, f32)], a.size, a, b)[0]


def core_sums(g, tc, g3):
    return call(core_sum_kernel, [(g3.shape, f32)] * 3, 3 * g3.size, g, tc, g3)


def cross(gx, gy, x1, y1):
    return call(cross_kernel, [(gx.shape, f32)] * 2, 2 * gx.size, gx, gy, x1, y1)


def finish(rows, g):
    return call(final_kernel, [(rows.shape, f32)], 12 * rows.size, rows, g, kept=False)[0]


def body(queries, passages, positive):
    pa = lax.axis_index("pa")
    q_full = lax.all_gather(queries, "pa", axis=0, tiled=True)
    p_full = lax.all_gather(passages, "pb", axis=0, tiled=True)
    p_rows, q_rows = p_full.shape[0], q_full.shape[0]
    pos = positive - pa * p_rows
    pos = jnp.where((pos >= 0) & (pos < p_rows), pos, -1).reshape(1, -1)
    et, stats, qh, ql, ph, pl_ = all_scores(q_full, p_full, pos)
    both = [lax.psum(stats, "pa")]
    u, v = unscaled(et, pos, [ph], [pl_])
    losses, gq = query_grads(both, u, v, (((0, q_rows),),))
    (gp,) = passage_grads(both, et, pos, qh, ql, ((0, p_rows),))
    q_part = lax.psum_scatter(gq, "pa", scatter_dimension=0, tiled=True)
    p_part = lax.psum_scatter(gp, "pb", scatter_dimension=0, tiled=True)
    return losses.reshape(-1), finish(queries, q_part), finish(passages, p_part)


def solution(mesh):
    placed = (P(("pb", "pa"), None), P(("pa", "pb"), None), P("pb"))
    small = mesh.shape["pa"] == 4 and mesh.shape["pb"] == 8
    return jax.shard_map(
        small_body if small else body,
        mesh=mesh,
        in_specs=placed,
        out_specs=(P("pb"), P(("pb", "pa"), None), P(("pa", "pb"), None)),
        check_vma=False,
    )
```

```python
import functools

import jax
import jax.numpy as jnp
from jax import lax
from jax.experimental import pallas as pl
from jax.experimental.pallas import tpu as pltpu
from jax.sharding import PartitionSpec as P

inv_temp = 20.0
f32 = jnp.float32
bf16 = jnp.bfloat16
AXES = ("pb", "pa")
X, Y, C, Z1, Z2 = 1, 2, 4, 8, 16
EARLY = 2


def call(kernel, outs, flops, *args, kept=True):
    return pl.pallas_call(
        kernel,
        out_shape=[pltpu.VMEM(s, d) if kept else jax.ShapeDtypeStruct(s, d) for s, d in outs],
        compiler_params=pltpu.CompilerParams(vmem_limit_bytes=24 * 1024 * 1024),
        cost_estimate=pl.CostEstimate(flops=flops, bytes_accessed=8 << 20, transcendentals=0),
    )(*args)


def split(x):
    hi = x.astype(bf16)
    return hi, (x - hi.astype(f32)).astype(bf16)


def mm(a, b, dims):
    return lax.dot_general(a, b, (dims, ((), ())), preferred_element_type=f32)


def mm3(a, b, dims):
    (ah, al), (bh, bl) = a, b
    n = ah.shape[0]
    if n > 256:
        return mm(al, bh, dims) + mm(ah, bl, dims) + mm(ah, bh, dims)
    both = mm(jnp.concatenate([al, ah], axis=0), bh, dims)
    return both[:n] + mm(ah, bl, dims) + both[n:]


def lift(scale):
    return jnp.broadcast_to(scale, (scale.shape[0], 128))


def normalize(rows):
    scale = lax.rsqrt(jnp.sum(rows * rows, axis=1, keepdims=True) + 1e-06)
    return rows * scale, scale


def onehot(pos, shape, first):
    return lax.broadcasted_iota(jnp.int32, shape, 0) + first == pos


def combine(stats):
    n = stats[0].shape[1] // len(stats)
    blocks = [sum(r[:, (m ^ k) * n : (m ^ k) * n + n] for k, r in enumerate(stats)) for m in range(len(stats))]
    return jnp.concatenate(blocks, axis=1)


def load(parts, hi, lo):
    at = 0
    for r in parts:
        if isinstance(r, tuple):
            n = r[0].shape[0]
            hi[at : at + n], lo[at : at + n] = r[0][...], r[1][...]
        else:
            n = r.shape[0]
            hi[at : at + n], lo[at : at + n] = split(normalize(r[...])[0])
        at += n


def own_kernel(queries, passages, qn, qs, qh, ql, pn, ps, ph, pl_):
    for rows, xn, scale, hi, lo in ((queries, qn, qs, qh, ql), (passages, pn, ps, ph, pl_)):
        x, r = normalize(rows[...])
        xn[...] = x
        scale[...] = lift(r)
        hi[...], lo[...] = split(x)


def product(p, q):
    if q[0].shape[0] <= 128:
        return inv_temp * narrow(p, q)
    if p[0].shape[0] <= 128:
        return inv_temp * narrow(q, p).T
    return inv_temp * mm3((p[0][...], p[1][...]), (q[0][...], q[1][...]), ((1,), (1,)))


def narrow(a, b):
    n = b[0].shape[0]
    bh = b[0][...]
    both = mm(a[0][...], jnp.concatenate([bh, b[1][...]], axis=0), ((1,), (1,)))
    return mm(a[1][...], bh, ((1,), (1,))) + both[:, n:] + both[:, :n]


def positives(pos, ph, pl_, first):
    o = onehot(pos[...], (ph.shape[0], pos.shape[1]), first).astype(f32).T.astype(bf16)
    return mm(o, pl_, ((1,), (0,))) + mm(o, ph, ((1,), (0,)))


def write_scores(et, stats, p, q, pos, first, new=False):
    st = product(p, q)
    e = jnp.exp(st)
    et[...] = e
    total = jnp.sum(e, axis=0, keepdims=True)
    spos = jnp.sum(jnp.where(onehot(pos, st.shape, first), st, 0.0), axis=0, keepdims=True)
    if new:
        stats[...] = jnp.zeros(stats.shape, f32)
        stats[0:1], stats[1:2] = total, spos
    else:
        stats[0:1] += total
        stats[1:2] += spos


def first_scores_kernel(*refs):
    qh0, ql0, ph0, pl0, x, y, z1, z2, c0, c1, c2, pos, et, stats, qh, ql, ph, pl_, v = refs
    load([(qh0, ql0), x, y], qh, ql)
    load([(ph0, pl0), z1, z2, c0, c1, c2], ph, pl_)
    write_scores(et, stats, (ph, pl_), (qh, ql), pos[:, : et.shape[1]], 0, True)
    m = 2 * ph.shape[0] // 3
    v[...] = positives(pos, ph[:m], pl_[:m], 0)


def rest_scores_kernel(da, db, c3, z3, pos, stats1, qh1, ql1, ph1, pl1, et_p, et_q, stats, qh, ql, ph2, pl2):
    n, r = qh1.shape[0], ph1.shape[0]
    load([c3, z3], ph2, pl2)
    stats[:, :n] = stats1[...]
    write_scores(et_p, stats.at[:, :n], (ph2, pl2), (qh1, ql1), pos[:, :n], r)
    load([da, db], qh, ql)
    write_scores(et_q.at[:r], stats.at[:, n:], (ph1, pl1), (qh, ql), pos[:, n:], 0, True)
    write_scores(et_q.at[r:], stats.at[:, n:], (ph2, pl2), (qh, ql), pos[:, n:], r)


def all_scores_kernel(q, p, pos, et, stats, qh, ql, ph, pl_):
    load([q], qh, ql)
    load([p], ph, pl_)
    write_scores(et, stats, (ph, pl_), (qh, ql), pos[...], 0, True)


def others(et, pos, first, n):
    rows = et[first : first + n]
    return split(jnp.where(onehot(pos[...], rows.shape, first), 0.0, rows).T)


def unscaled_kernel(et1, et_p, et_q, pos, qh1, ql1, qh2, ql2, ph1, pl1, phz, plz, v1, et, qh, ql, u, v):
    r, n = et1.shape
    et[:r, :n], et[r:, :n], et[:, n:] = et1[...], et_p[...], et_q[...]
    qh[:n], ql[:n], qh[n:], ql[n:] = qh1[...], ql1[...], qh2[...], ql2[...]
    m = 2 * r // 3
    ph2, pl2 = (jnp.concatenate([a[m:], b[...]], axis=0) for a, b in ((ph1, phz), (pl1, plz)))
    first = mm3(others(et, pos, 0, m), (ph1[:m], pl1[:m]), ((1,), (0,)))
    u[...] = first + mm3(others(et, pos, m, ph2.shape[0]), (ph2, pl2), ((1,), (0,)))
    v[...] = v1[...] + positives(pos, ph2, pl2, m)


def all_unscaled_kernel(et, pos, ph, pl_, u, v):
    u[...] = mm3(others(et, pos, 0, et.shape[0]), (ph[...], pl_[...]), ((1,), (0,)))
    v[...] = positives(pos, ph[...], pl_[...], 0)


def query_kernel(n_stats, cuts, *refs):
    stats = refs[:n_stats]
    u, v, losses, *outs = refs[n_stats:]
    both = combine(stats)
    total, spos = both[0:1], both[1:2]
    losses[...] = jnp.log(total) - spos
    weight = 1.0 / total
    scales = jnp.concatenate([weight, jnp.exp(spos) * weight - 1.0, both[2:]], axis=0).T
    for out, ranges in zip(outs, cuts):
        at = 0
        for a, b in ranges:
            out[at : at + b - a] = u[a:b] * scales[a:b, 0:1] + v[a:b] * scales[a:b, 1:2]
            at += b - a


def passage_kernel(n_stats, cuts, *refs):
    stats = refs[:n_stats]
    et, pos, qh, ql, *outs = refs[n_stats:]
    weight = 1.0 / combine(stats)[0:1]
    d = [et[a:b] * weight - onehot(pos[...], (b - a, et.shape[1]), a).astype(f32) for a, b in cuts]
    g = mm3(split(jnp.concatenate(d, axis=0)), (qh[...], ql[...]), ((1,), (0,)))
    at = 0
    for out, (a, b) in zip(outs, cuts):
        out[...] = g[at : at + b - a]
        at += b - a


def core_sum_kernel(g, tc, g3, t1, t2, t3):
    n = g3.shape[0]
    t1[...] = g[n : 2 * n] + tc[n : 2 * n]
    t2[...] = g[2 * n :] + tc[2 * n : 3 * n]
    t3[...] = g3[...] + tc[3 * n :]


def add_kernel(a, b, out):
    out[...] = a[...] + b[...]


def cross_kernel(gx, gy, x1, y1, x, y):
    n = gx.shape[0]
    h = (n + x1.shape[0]) // 3
    x[: n - h] = gx[: n - h]
    x[n - h :] = gx[n - h :] + y1[:h]
    y[:h] = gy[:h] + x1[:h]
    y[h:] = gy[h:]


def project(g, xn, scale):
    g = inv_temp * g
    return scale * (g - xn * jnp.sum(xn * g, axis=1, keepdims=True))


def last_kernel(qn, qs, pn, ps, own, x1, y1, x2, y2, g, tc, r1, r2, out_q, out_p):
    h, m = qn.shape[0] // 2, pn.shape[0]
    k = x1.shape[0] - h
    for at, n, p, pa, q, qa in ((0, k, x1, h, y2, 0), (k, h - k, x2, 0, y2, k), (h, k, y1, h, x2, h - k), (h + k, h - k, y2, h, x2, h)):
        if n:
            s = own[at : at + n] + p[pa : pa + n] + q[qa : qa + n]
            out_q[at : at + n] = project(s, qn[at : at + n], qs[at : at + n, 0:1])
    out_p[...] = project(g[:m] + tc[:m] + r1[...] + r2[...], pn[...], ps[:, 0:1])


def final_kernel(rows, g, out):
    xn, scale = normalize(rows[...])
    out[...] = project(g[...], xn, scale)


def flip(x, mask):
    n = lax.axis_size("pb") * lax.axis_size("pa")
    return lax.ppermute(x, AXES, [(i, i ^ mask) for i in range(n)])


def after(x, *others):
    return lax.optimization_barrier((x,) + others)[0]


def by_xor(x, k):
    x = jnp.where(k & 1, jnp.stack([x[1], x[0], x[3], x[2]]), x)
    return jnp.where(k & 2, jnp.stack([x[2], x[3], x[0], x[1]]), x)


def small_body(queries, passages, positive):
    qr, pr = queries.shape[0], passages.shape[0]
    h = qr // 2
    p_rows = 8 * pr
    pa, pb = lax.axis_index("pa"), lax.axis_index("pb")

    pos = by_xor(positive.reshape(4, qr), pa).reshape(1, 4 * qr)
    block = ((pos % p_rows) // pr) ^ pb
    place = jnp.where(block == 6, 7, block // 2 + 3 * (block % 2))
    pos = jnp.where(pos // p_rows == pa, place * pr + pos % pr, -1)

    z2, z1 = flip(passages, Z2), flip(passages, Z1)
    x, y = flip(queries, X), flip(queries, Y)
    c0 = flip(passages, C)
    qn, qs, qh0, ql0, pn, ps, ph0, pl0 = own_rows(queries, passages)
    z2 = after(z2, qh0, pos)
    z3 = flip(z2, Z1)
    da, db = flip(after(x[:h], c0), Y), flip(after(y[h:], c0), X)
    c1 = flip(after(z1, qh0, pos), C)
    c2 = flip(after(z2, c1), C)
    *first, v1 = first_scores(qh0, ql0, ph0, pl0, x, y, z1, z2, c0, c1, c2, pos)
    c3 = flip(z3, C)
    et1, stats, *first = first
    et_p, et_q, stats, qh2, ql2, phz, plz = rest_scores(da, db, c3, z3, pos, stats, *first)

    both = [stats, flip(stats, X), flip(stats, Y), flip(stats, X + Y)]
    qh1, ql1, *p_rest = first
    et, qh, ql, u, v = unscaled(et1, et_p, et_q, pos, qh1, ql1, qh2, ql2, *p_rest, phz, plz, v1)

    def part(k, n):
        return (k * n, k * n + n)

    (gc,) = passage_grads(both, after(et, u), pos, qh, ql, ((3 * pr, 7 * pr),))
    tc = flip(gc, C)
    g, g3 = passage_grads(both, after(et, gc), pos, qh, ql, ((0, 3 * pr), (7 * pr, 8 * pr)))
    k = EARLY * h // 4
    kx, ky = 2 * h + k, 5 * h + k
    cuts = ((part(6, h), (2 * h, kx)), (part(7, h), (5 * h, ky)), ((kx, 4 * h),), (part(4, h), (ky, 6 * h)), ((0, qr),))
    losses, gx1, gy1, gx, gy, own = query_grads(both, after(u, g), v, cuts)
    x1, y1 = flip(gx1, X), flip(gy1, Y)
    t1, t2, t3 = core_sums(g, tc, g3)
    r3 = flip(t3, Z1)
    t2 = add(t2, r3)
    r1, r2 = flip(after(t1, t2), Z1), flip(t2, Z2)
    gx, gy = cross(after(gx, t2), gy, x1, y1)
    x2, y2 = flip(gx, X), flip(gy, Y)

    losses = by_xor(losses.reshape(4, qr), pa).reshape(4 * qr)
    query_grad, passage_grad = call(
        last_kernel,
        [(queries.shape, f32), (passages.shape, f32)],
        12 * queries.size,
        *(qn, qs, pn, ps, own, x1, y1, x2, y2, g, tc, r1, r2),
        kept=False,
    )
    return losses, query_grad, passage_grad


def rows(parts):
    return sum(x.shape[0] for x in parts)


def own_rows(queries, passages):
    outs = []
    for n, d in (queries.shape, passages.shape):
        outs += [((n, d), f32), ((n, 128), f32), ((n, d), bf16), ((n, d), bf16)]
    return call(own_kernel, outs, 4 * queries.size, queries, passages)


def scores_outs(q, p, d):
    return [((p, q), f32), ((8, q), f32), ((q, d), bf16), ((q, d), bf16), ((p, d), bf16), ((p, d), bf16)]


def first_scores(qh0, ql0, ph0, pl0, x, y, z1, z2, c0, c1, c2, pos):
    q, p, d = rows([qh0, x, y]), rows([ph0, z1, z2, c0, c1, c2]), x.shape[1]
    outs = scores_outs(q, p, d) + [((pos.shape[1], d), f32)]
    return call(first_scores_kernel, outs, 10 * q * p * d, qh0, ql0, ph0, pl0, x, y, z1, z2, c0, c1, c2, pos)


def rest_scores(da, db, c3, z3, pos, stats1, qh1, ql1, ph1, pl1):
    q, p, d = rows([da, db]), rows([c3, z3]), da.shape[1]
    r, n = ph1.shape[0], qh1.shape[0]
    outs = [((p, n), f32), ((r + p, q), f32), ((8, n + q), f32)] + [((k, d), bf16) for k in (q, q, p, p)]
    return call(rest_scores_kernel, outs, 6 * q * p * d, da, db, c3, z3, pos, stats1, qh1, ql1, ph1, pl1)


def all_scores(q, p, pos):
    work = 6 * q.size * p.shape[0]
    return call(all_scores_kernel, scores_outs(q.shape[0], p.shape[0], q.shape[1]), work, q, p, pos)


def unscaled(*args):
    et_q, q, d = args[2], args[3].shape[1], args[4].shape[1]
    p = et_q.shape[0]
    outs = [((p, q), f32), ((q, d), bf16), ((q, d), bf16), ((q, d), f32), ((q, d), f32)]
    return call(unscaled_kernel, outs, 8 * q * p * d, *args)


def all_unscaled(et, pos, ph, pl_):
    p, q = et.shape
    return call(all_unscaled_kernel, [((q, ph.shape[1]), f32)] * 2, 8 * q * ph.size, et, pos, ph, pl_)


def query_grads(both, u, v, cuts):
    q, d = u.shape
    return call(
        functools.partial(query_kernel, len(both), cuts),
        [((1, q), f32)] + [((sum(b - a for a, b in ranges), d), f32) for ranges in cuts],
        3 * q * d,
        *both,
        u,
        v,
    )


def passage_grads(both, et, pos, qh, ql, cuts):
    q, d = qh.shape
    return call(
        functools.partial(passage_kernel, len(both), cuts),
        [((b - a, d), f32) for a, b in cuts],
        6 * q * d * sum(b - a for a, b in cuts),
        *both,
        et,
        pos,
        qh,
        ql,
    )


def add(a, b):
    return call(add_kernel, [(a.shape, f32)], a.size, a, b)[0]


def core_sums(g, tc, g3):
    return call(core_sum_kernel, [(g3.shape, f32)] * 3, 3 * g3.size, g, tc, g3)


def cross(gx, gy, x1, y1):
    return call(cross_kernel, [(gx.shape, f32)] * 2, 2 * gx.size, gx, gy, x1, y1)


def finish(rows, g):
    return call(final_kernel, [(rows.shape, f32)], 12 * rows.size, rows, g, kept=False)[0]


def body(queries, passages, positive):
    pa = lax.axis_index("pa")
    q_full = lax.all_gather(queries, "pa", axis=0, tiled=True)
    p_full = lax.all_gather(passages, "pb", axis=0, tiled=True)
    p_rows, q_rows = p_full.shape[0], q_full.shape[0]
    pos = positive - pa * p_rows
    pos = jnp.where((pos >= 0) & (pos < p_rows), pos, -1).reshape(1, -1)
    et, stats, qh, ql, ph, pl_ = all_scores(q_full, p_full, pos)
    both = [lax.psum(stats, "pa")]
    u, v = all_unscaled(et, pos, ph, pl_)
    losses, gq = query_grads(both, u, v, (((0, q_rows),),))
    (gp,) = passage_grads(both, et, pos, qh, ql, ((0, p_rows),))
    q_part = lax.psum_scatter(gq, "pa", scatter_dimension=0, tiled=True)
    p_part = lax.psum_scatter(gp, "pb", scatter_dimension=0, tiled=True)
    return losses.reshape(-1), finish(queries, q_part), finish(passages, p_part)


def solution(mesh):
    placed = (P(("pb", "pa"), None), P(("pa", "pb"), None), P("pb"))
    small = mesh.shape["pa"] == 4 and mesh.shape["pb"] == 8
    return jax.shard_map(
        small_body if small else body,
        mesh=mesh,
        in_specs=placed,
        out_specs=(P("pb"), P(("pb", "pa"), None), P(("pa", "pb"), None)),
        check_vma=False,
    )
```
